32 devices in a mesh: seq: 4 (over z), section: 2 (over core), batch: 4 (over y, x).
Axes of the slice: x: 2, y: 2, z: 4, core: 2. Of those that a mesh axis runs over, the one named last changes fastest.
Arguments:
- features: bfloat16 [4, 16384, 768], P('batch', 'seq'), may hold values from -6 to 6
- dilated_tap_weight: bfloat16 [3, 768, 768], P(None, None, 'section'), may hold values from -0.125 to 0.125
- strided_weight: bfloat16 [2, 768, 1536], P(None, None, 'section'), may hold values from -0.15625 to 0.15625
- norm_gain: float32 [1536], replicated, may hold values from 0.1 to 1.9
- query_weight: bfloat16 [1536, 1024], P(None, 'section'), may hold values from -0.15625 to 0.15625
- key_weight: bfloat16 [1536, 1024], P(None, 'section'), may hold values from -0.15625 to 0.15625
- value_weight: bfloat16 [1536, 1536], P(None, 'section'), may hold values from -0.15625 to 0.15625
- output_weight: bfloat16 [1536, 1536], P('section'), may hold values from -0.15625 to 0.15625
- position_bias: float32 [4, 8, 128, 128], P('batch', 'section', 'seq'), may hold values from -4 to 320
- interval_start: int32 [4, 128], P('batch', 'seq'), may hold values from 0 to 126, as said below
- interval_end: int32 [4, 128], P('batch', 'seq'), may hold values from 2 to 128, as said below
- cotangent: bfloat16 [4, 128, 1536], P('batch', 'seq'), may hold values from -0.19921875 to 0.19921875
Outputs:
- layer_out: bfloat16 [4, 128, 1536], P('batch', 'seq', 'section')
- output_grad: float32 [1536, 1536], P('section')
The draws below stay inside these ranges and needn't reach their ends.
Inputs may be any that keep to these rules, and one draw needn't show every extreme that they name: interval_start[b, i] <= max(i - 1, 0): each query sees itself and the position before it. interval_end[b, i] >= min(i + 2, 128): each query sees the position after it.
All inputs are finite; a program needn't handle non-finite values.
Results may differ from the reference program's by a relative error of at most 0.02.
Values may be sent and summed in bfloat16 or wider, within the bound.
A program may use at most 128 MiB of HBM per device.

```python
import jax
import jax.numpy as jnp
from jax import lax

C1 = 768
C2 = 1536
HEADS = 8
KEY = 128
VAL = 192
POOL = 128
DILATION_STEP = 8
SLAB_BASE_PAIRS = 16384
POS = 128
BATCH = 4


def interval_pair(key):
    first_key, second_key = jax.random.split(jax.random.fold_in(key, 11))
    reach_low = jax.random.randint(first_key, (BATCH, POS), 0, POS // 2 + 1)
    reach_high = jax.random.randint(second_key, (BATCH, POS), 0, POS // 2 + 1)
    positions = jnp.arange(POS, dtype=jnp.int32)[None, :]
    lower = jnp.maximum(positions - 1 - reach_low, 0)
    upper = jnp.minimum(positions + 2 + reach_high, POS)
    return (lower.astype(jnp.int32), upper.astype(jnp.int32))


def draw_interval_start(key, part):
    return interval_pair(key)[0]


def draw_interval_end(key, part):
    return interval_pair(key)[1]


def draw_position_bias(key, part):
    first_key = jax.random.fold_in(jax.random.fold_in(key, 23), 0)
    shape = (BATCH, HEADS, POS, POS)
    return jnp.clip(jax.random.normal(first_key, shape, jnp.float32), -4.0, 4.0)


def shard_levels(key, shape, shards, smallest, high):
    def one(position, blocks):
        draws = jax.random.uniform(jax.random.fold_in(jax.random.fold_in(key, 6), position), (blocks,), jnp.float32, smallest / len(shards), high / len(shards))
        return jnp.repeat(jnp.exp(draws), shape[position] // blocks).reshape((-1,) + (1,) * (len(shape) - position - 1))

    factor_of = one(*shards[0])
    for cut in shards[1:]:
        factor_of = factor_of * one(*cut)
    return factor_of


def normal_values(key, extent, width, reach, pieces=(), kind=jnp.bfloat16):
    values = jax.random.normal(key, extent, jnp.float32) * width
    if len(pieces) > 0:
        values = shard_levels(key, extent, pieces, -0.22, 0.18) * values
    return jnp.clip(values, min=-reach, max=reach).astype(kind)


def setup_inputs(seed: int = 0) -> dict:
    arg_keys = jax.random.split(jax.random.key(seed), 13)
    return {
        "features": normal_values(arg_keys[0], (BATCH, SLAB_BASE_PAIRS, C1), 1.0, 6.0, ((0, 4), (1, 4))),
        "dilated_tap_weight": normal_values(arg_keys[1], (3, C1, C1), (3 * C1) ** -0.5, 0.125, ((2, 2),)),
        "strided_weight": normal_values(arg_keys[2], (2, C1, C2), (2 * C1) ** -0.5, 0.15625, ((2, 2),)),
        "norm_gain": jnp.clip(1.0 + 0.18 * jax.random.normal(arg_keys[3], (C2,), jnp.float32), 0.1, 1.9),
        "query_weight": normal_values(arg_keys[4], (C2, HEADS * KEY), C2 ** -0.5, 0.15625, ((1, 2),)),
        "key_weight": normal_values(arg_keys[5], (C2, HEADS * KEY), C2 ** -0.5, 0.15625, ((1, 2),)),
        "value_weight": normal_values(arg_keys[6], (C2, HEADS * VAL), C2 ** -0.5, 0.15625, ((1, 2),)),
        "output_weight": normal_values(arg_keys[7], (HEADS * VAL, C2), (HEADS * VAL) ** -0.5, 0.15625, ((0, 2),)),
        "position_bias": draw_position_bias(jax.random.fold_in(arg_keys[12], 71), 0),
        "interval_start": draw_interval_start(jax.random.fold_in(arg_keys[12], 71), 0),
        "interval_end": draw_interval_end(jax.random.fold_in(arg_keys[12], 71), 0),
        "cotangent": normal_values(arg_keys[11], (BATCH, POS, C2), 0.03, 0.19921875, ((0, 4), (1, 4))),
    }


def one_slab(input_rows, bias_s, start_s, end_s, cot_s, dilated_tap_weight, strided_weight, norm_gain, query_weight, key_weight, value_weight, output_weight):
    padded_input = jnp.pad(input_rows, ((DILATION_STEP, DILATION_STEP), (0, 0)))
    before_activation = jnp.dot(padded_input[0:SLAB_BASE_PAIRS], dilated_tap_weight[0], preferred_element_type=jnp.float32)
    before_activation = before_activation + jnp.dot(padded_input[DILATION_STEP:DILATION_STEP + SLAB_BASE_PAIRS], dilated_tap_weight[1], preferred_element_type=jnp.float32)
    before_activation = before_activation + jnp.dot(padded_input[2 * DILATION_STEP:2 * DILATION_STEP + SLAB_BASE_PAIRS], dilated_tap_weight[2], preferred_element_type=jnp.float32)
    hidden = (input_rows.astype(jnp.float32) + jax.nn.gelu(before_activation)).astype(jnp.bfloat16)
    strided = jnp.dot(hidden.reshape(SLAB_BASE_PAIRS // 2, 2 * C1), strided_weight.reshape(2 * C1, C2), preferred_element_type=jnp.float32)
    pooled = strided.reshape(POS, POOL // 2, C2).max(axis=1).astype(jnp.bfloat16)
    values_f = pooled.astype(jnp.float32)
    centred = values_f - lax.optimization_barrier(jnp.mean(values_f, axis=1, keepdims=True))
    spread = lax.optimization_barrier(jnp.mean(centred * centred, axis=1, keepdims=True))
    normed = centred * lax.rsqrt(spread + 1e-05) * norm_gain
    inputs_b = normed.astype(jnp.bfloat16)
    query = (jnp.dot(inputs_b, query_weight, preferred_element_type=jnp.float32) * KEY ** (-0.5)).astype(jnp.bfloat16)
    keyed = jnp.dot(inputs_b, key_weight, preferred_element_type=jnp.float32).astype(jnp.bfloat16)
    valued = jnp.dot(inputs_b, value_weight, preferred_element_type=jnp.float32).astype(jnp.bfloat16)
    query3 = query.reshape(POS, HEADS, KEY).astype(jnp.float32)
    key3 = keyed.reshape(POS, HEADS, KEY).astype(jnp.float32)
    value3 = valued.reshape(POS, HEADS, VAL).astype(jnp.float32)
    scores = jnp.einsum('qhd,khd->hqk', query3, key3) + bias_s
    positions = jnp.arange(POS, dtype=jnp.int32)
    visible = (positions[None, :] >= start_s[:, None]) & (positions[None, :] < end_s[:, None])
    scores = jnp.where(visible[None], scores, jnp.float32(-1e+30))
    highest = lax.optimization_barrier(jnp.max(scores, axis=2, keepdims=True))
    weight_arrays = jnp.where(visible[None], jnp.exp(scores - highest), jnp.float32(0.0))
    total = lax.optimization_barrier(jnp.sum(weight_arrays, axis=2))
    rounded = lax.optimization_barrier(weight_arrays.astype(jnp.bfloat16)).astype(jnp.float32)
    summed = jnp.einsum('hqk,khd->hqd', rounded, value3) / total[:, :, None]
    attended = summed.transpose(1, 0, 2).reshape(POS, HEADS * VAL).astype(jnp.bfloat16)
    layer_out = (normed + jnp.dot(attended, output_weight, preferred_element_type=jnp.float32)).astype(jnp.bfloat16)
    grad_term = jnp.dot(attended.T, cot_s, preferred_element_type=jnp.float32)
    return (layer_out, grad_term)

def reference(features, dilated_tap_weight, strided_weight, norm_gain, query_weight, key_weight, value_weight, output_weight, position_bias, interval_start, interval_end, cotangent):

    def per_slab(index):
        return one_slab(features[index], position_bias[index], interval_start[index], interval_end[index], cotangent[index], dilated_tap_weight, strided_weight, norm_gain, query_weight, key_weight, value_weight, output_weight)
    outputs, grads = lax.map(per_slab, jnp.arange(BATCH, dtype=jnp.int32))
    return (outputs, lax.optimization_barrier(jnp.sum(grads, axis=0)))
```

```python
import jax
import jax.numpy as jnp
from jax import lax
from jax.sharding import PartitionSpec as P

KEY = 128
VAL = 192
POOL = 128
DILATION_STEP = 8


def padded(shard, sides, width):
    for axis, dim in sides:
        size, length = (lax.axis_size(axis), shard.shape[dim])
        up = [(i, (i + 1) % size) for i in range(size - 1)]
        down = [(j, i) for i, j in up]
        last = lax.slice_in_dim(shard, length - width, length, axis=dim)
        leading = lax.slice_in_dim(shard, 0, width, axis=dim)
        before = lax.ppermute(last, axis, up)
        after = lax.ppermute(leading, axis, down)
        shard = jnp.concatenate([before, shard, after], axis=dim)
    return shard


def dilated_block(padded_input, local_sequence, weight_arrays, begin):
    sequence_length = local_sequence.shape[0]
    columns = weight_arrays.shape[2]
    before_activation = jnp.dot(
        padded_input[0:sequence_length], weight_arrays[0], preferred_element_type=jnp.float32
    )
    before_activation = before_activation + jnp.dot(
        padded_input[DILATION_STEP : DILATION_STEP + sequence_length],
        weight_arrays[1],
        preferred_element_type=jnp.float32,
    )
    before_activation = before_activation + jnp.dot(
        padded_input[2 * DILATION_STEP : 2 * DILATION_STEP + sequence_length],
        weight_arrays[2],
        preferred_element_type=jnp.float32,
    )
    own_cols = lax.dynamic_slice_in_dim(local_sequence, begin, columns, 1)
    return (own_cols.astype(jnp.float32) + jax.nn.gelu(before_activation)).astype(jnp.bfloat16)


def shards(
    features,
    dilated_tap_weight,
    strided_weight,
    norm_gain,
    query_weight,
    key_weight,
    value_weight,
    output_weight,
    position_bias,
    interval_start,
    interval_end,
    cotangent,
):
    cotangent_all = lax.all_gather(cotangent[0], ("batch", "seq"), axis=0, tiled=True)
    local_sequence = features[0]
    sequence_length = local_sequence.shape[0]
    padded_input = padded(local_sequence, (("seq", 0),), DILATION_STEP)
    out_cols = strided_weight.shape[2]
    hidden = dilated_block(
        padded_input,
        local_sequence,
        dilated_tap_weight,
        lax.axis_index("section") * dilated_tap_weight.shape[2],
    )
    piece = lax.all_gather(hidden, "section", axis=1, tiled=True)
    width = piece.shape[1]
    paired = piece.reshape(sequence_length // 2, 2 * width)
    taps = strided_weight.reshape(2 * width, out_cols)
    strided = jnp.dot(paired, taps, preferred_element_type=jnp.float32)
    pooled = (
        strided.reshape(sequence_length // POOL, POOL // 2, out_cols)
        .max(axis=1)
        .astype(jnp.bfloat16)
    )
    gathered = lax.all_gather(pooled, "section", axis=1, tiled=True)
    values_f = gathered.astype(jnp.float32)
    centred = values_f - jnp.mean(values_f, axis=1, keepdims=True)
    spread = jnp.mean(centred * centred, axis=1, keepdims=True)
    normed = centred * lax.rsqrt(spread + 1e-05) * norm_gain
    inputs_b = normed.astype(jnp.bfloat16)
    query = (
        jnp.dot(inputs_b, query_weight, preferred_element_type=jnp.float32) * KEY ** (-0.5)
    ).astype(jnp.bfloat16)
    keyed = jnp.dot(inputs_b, key_weight, preferred_element_type=jnp.float32).astype(jnp.bfloat16)
    valued = jnp.dot(inputs_b, value_weight, preferred_element_type=jnp.float32).astype(
        jnp.bfloat16
    )
    rows = query.shape[0]
    heads_local = query.shape[1] // KEY
    query3 = query.reshape(rows, heads_local, KEY)
    bias_local = position_bias[0]
    lower = interval_start[0]
    upper = interval_end[0]
    best = jnp.full((heads_local, rows), -1e30, jnp.float32)
    key_piece = lax.all_gather(keyed, "seq", axis=0, tiled=True)
    value_piece = lax.all_gather(valued, "seq", axis=0, tiled=True)
    count = key_piece.shape[0]
    key3 = key_piece.reshape(count, heads_local, KEY)
    value3 = value_piece.reshape(count, heads_local, VAL)
    scores = jnp.einsum("qhd,khd->hqk", query3, key3, preferred_element_type=jnp.float32)
    scores = scores + bias_local
    positions = jnp.arange(count, dtype=jnp.int32)
    visible = (positions[None, :] >= lower[:, None]) & (positions[None, :] < upper[:, None])
    scores = jnp.where(visible[None], scores, jnp.float32(-1e30))
    newest = jnp.maximum(best, jnp.max(scores, axis=2))
    weight_arrays = jnp.where(visible[None], jnp.exp(scores - newest[:, :, None]), jnp.float32(0.0))
    weight_sum = jnp.sum(weight_arrays, axis=2)
    accum = jnp.einsum(
        "hqk,khd->hqd",
        weight_arrays.astype(jnp.bfloat16),
        value3,
        preferred_element_type=jnp.float32,
    )
    final_best, weight_sum, accum = (newest, weight_sum, accum)
    attended = (
        (accum / weight_sum[:, :, None])
        .transpose(1, 0, 2)
        .reshape(rows, heads_local * VAL)
        .astype(jnp.bfloat16)
    )
    projected = jnp.dot(attended, output_weight, preferred_element_type=jnp.float32)
    mixed = lax.psum_scatter(projected, "section", scatter_dimension=1, tiled=True)
    own_norm = lax.dynamic_slice_in_dim(normed, lax.axis_index("section") * out_cols, out_cols, 1)
    layer_out = (own_norm + mixed).astype(jnp.bfloat16)[None]
    attended_all = lax.all_gather(attended, ("batch", "seq"), axis=0, tiled=True)
    output_grad = lax.dot_general(
        attended_all,
        cotangent_all,
        (((0,), (0,)), ((), ())),
        preferred_element_type=jnp.float32,
    )
    return (layer_out, output_grad)


def solution(mesh):
    return jax.shard_map(
        shards,
        mesh=mesh,
        in_specs=(
            P("batch", "seq", None),
            P(None, None, "section"),
            P(None, None, "section"),
            P(),
            P(None, "section"),
            P(None, "section"),
            P(None, "section"),
            P("section", None),
            P("batch", "section", "seq", None),
            P("batch", "seq"),
            P("batch", "seq"),
            P("batch", "seq", None),
        ),
        out_specs=(P("batch", "seq", "section"), P("section", None)),
        check_vma=False,
    )
```

```python
import functools

import jax
import jax.numpy as jnp
from jax import lax
from jax.experimental import pallas as pl
from jax.experimental.pallas import tpu as pltpu
from jax.sharding import PartitionSpec as P

KEY = 128
VAL = 192
POOL = 128
STEP = 8
EDGE = 16
MESH = pl.DeviceIdType.MESH
LIMIT = 56 * 1024 * 1024


def conv_kernel(
    nseq, features, dil, strd, out, x, wd, ws, hs, hp, pooled, local_sem, send_sem, recv_sem
):
    s = lax.axis_index("seq")
    c = lax.axis_index("section")
    b = lax.axis_index("batch")
    length, width = features.shape
    half_rows = length // 2
    part = dil.shape[1]
    cols = strd.shape[1]
    peer = (s, 1 - c, b)
    after = (lax.rem(s + 1, nseq), c, b)
    before = (lax.rem(s + nseq - 1, nseq), c, b)
    halo_target = (lax.rem(s + 1 - 2 * c + nseq, nseq), c, b)

    load_x = pltpu.make_async_copy(
        features.at[pl.ds(pl.multiple_of(c * (half_rows - EDGE), EDGE), half_rows + EDGE)],
        x.at[pl.ds(pl.multiple_of(EDGE * (1 - c), EDGE), half_rows + EDGE)],
        local_sem.at[0],
    )
    load_d = pltpu.make_async_copy(dil, wd.at[0], local_sem.at[1])
    load_s = pltpu.make_async_copy(strd, ws.at[0], local_sem.at[2])
    load_d.start()
    load_x.start()

    barrier = pltpu.get_barrier_semaphore()
    for device in (peer, after, before):
        pl.semaphore_signal(barrier, inc=1, device_id=device, device_id_type=MESH)
    pl.semaphore_wait(barrier, 3)

    edge_row = pl.multiple_of(c * (half_rows + EDGE), EDGE)
    halo = pltpu.make_async_remote_copy(
        src_ref=features.at[pl.ds(pl.multiple_of((1 - c) * (length - EDGE), EDGE), EDGE)],
        dst_ref=x.at[pl.ds(edge_row, EDGE)],
        send_sem=send_sem.at[0],
        recv_sem=recv_sem.at[0],
        device_id=halo_target,
        device_id_type=MESH,
    )
    send_d = pltpu.make_async_remote_copy(
        src_ref=dil,
        dst_ref=wd.at[1],
        send_sem=send_sem.at[1],
        recv_sem=recv_sem.at[1],
        device_id=peer,
        device_id_type=MESH,
    )
    send_s = pltpu.make_async_remote_copy(
        src_ref=strd,
        dst_ref=ws.at[1],
        send_sem=send_sem.at[2],
        recv_sem=recv_sem.at[2],
        device_id=peer,
        device_id_type=MESH,
    )
    halo.start()
    send_d.start()
    send_s.start()
    load_s.start()

    load_x.wait()
    load_d.wait()
    halo.wait()
    outside = ((c == 0) & (s == 0)) | ((c == 1) & (s == nseq - 1))
    keep = jnp.where(outside, 0.0, 1.0).astype(jnp.float32)
    edge = x[pl.ds(edge_row, EDGE), :].astype(jnp.float32) * keep
    x[pl.ds(edge_row, EDGE), :] = edge.astype(jnp.bfloat16)

    chunk = hs.shape[2]
    lane_blocks = part // 128

    def dilated(slot, half):
        first = pl.multiple_of(half * part, 128)

        def body(i, carry):
            row = pl.multiple_of(i * chunk, chunk)
            block = x[pl.ds(row, chunk + 2 * EDGE), :]
            taps = jnp.concatenate(
                [block[EDGE + d : EDGE + d + chunk] for d in (-STEP, 0, STEP)], axis=1
            )
            preact = jnp.dot(taps, wd[slot], preferred_element_type=jnp.float32)
            own = x[pl.ds(row + EDGE, chunk), pl.ds(first, part)].astype(jnp.float32)
            hidden = own + jax.nn.gelu(preact)
            at = lax.rem(i, 2)
            for j in range(lane_blocks):
                hs[at, j] = hidden[:, 128 * j : 128 * (j + 1)]
            target = pl.multiple_of(i * (chunk // 2), chunk // 2)
            for parity in range(2):
                for j in range(lane_blocks):
                    lane = pl.multiple_of(first + parity * width + 128 * j, 128)
                    hp[pl.ds(target, chunk // 2), pl.ds(lane, 128)] = hs[
                        at, j, pl.ds(parity, chunk // 2, 2), :
                    ].astype(jnp.bfloat16)
            return carry

        lax.fori_loop(0, half_rows // chunk, body, 0, unroll=2)

    def strided(slot, half):
        rows = 8 * (POOL // 2)
        block_cols = 256
        per = cols // block_cols

        def body(k, carry):
            i, n = k // per, lax.rem(k, per)
            lane = pl.multiple_of(n * block_cols, block_cols)
            product = jnp.dot(
                hp[pl.ds(pl.multiple_of(i * rows, rows), rows), :],
                ws[slot, :, pl.ds(lane, block_cols)],
                preferred_element_type=jnp.float32,
            )
            best = product.reshape(8, POOL // 2, block_cols).max(axis=1)
            pooled[
                pl.ds(pl.multiple_of(i * 8, 8), 8),
                pl.ds(pl.multiple_of(half * cols + lane, 128), block_cols),
            ] = best
            return carry

        lax.fori_loop(0, half_rows // 2 // rows * per, body, 0)

    dilated(0, c)
    send_d.wait()
    dilated(1, 1 - c)
    load_s.wait()
    strided(0, c)
    send_s.wait()
    strided(1, 1 - c)
    out[...] = pooled[...].astype(jnp.bfloat16)


def conv(nseq, features, dil, strd):
    length, width = features.shape
    part = dil.shape[1]
    cols = strd.shape[1]
    rows = length // 2 // POOL
    chunk = 256
    hbm = pl.BlockSpec(memory_space=pl.ANY)
    return pl.pallas_call(
        functools.partial(conv_kernel, nseq),
        out_shape=jax.ShapeDtypeStruct((rows, 2 * cols), jnp.bfloat16),
        in_specs=[hbm, hbm, hbm],
        out_specs=pl.BlockSpec(memory_space=pltpu.VMEM),
        scratch_shapes=[
            pltpu.VMEM((length // 2 + 2 * EDGE, width), jnp.bfloat16),
            pltpu.VMEM((2,) + dil.shape, jnp.bfloat16),
            pltpu.VMEM((2,) + strd.shape, jnp.bfloat16),
            pltpu.VMEM((2, part // 128, chunk, 128), jnp.float32),
            pltpu.VMEM((length // 4, 2 * width), jnp.bfloat16),
            pltpu.VMEM((rows, 2 * cols), jnp.float32),
            pltpu.SemaphoreType.DMA((3,)),
            pltpu.SemaphoreType.DMA((3,)),
            pltpu.SemaphoreType.DMA((3,)),
        ],
        compiler_params=pltpu.CompilerParams(
            collective_id=0, has_side_effects=True, vmem_limit_bytes=LIMIT
        ),
        cost_estimate=pl.CostEstimate(
            flops=12_000_000_000, bytes_accessed=8_000_000, transcendentals=1_600_000
        ),
    )(features, dil, strd)


def attention_kernel(
    nseq,
    nbatch,
    pooled,
    gain,
    query_w,
    key_w,
    value_w,
    output_w,
    bias,
    lower,
    upper,
    layer_out,
    att,
    pool2,
    wq,
    wk,
    wv,
    wo,
    kv,
    proj,
    other,
    local_sem,
    pair_send,
    pair_recv,
    kv_send,
    kv_recv,
    att_send,
    att_recv,
):
    s = lax.axis_index("seq")
    c = lax.axis_index("section")
    b = lax.axis_index("batch")
    total = nseq * nbatch
    me = b * nseq + s
    half_rows = pooled.shape[0]
    rows = 2 * half_rows
    key_cols = key_w.shape[1]
    val_cols = value_w.shape[1]
    heads = key_cols // KEY
    out_cols = layer_out.shape[1]
    peer = (s, 1 - c, b)

    loads = [
        pltpu.make_async_copy(src, dst, local_sem.at[k])
        for k, (src, dst) in enumerate(
            ((key_w, wk), (value_w, wv), (query_w, wq), (output_w, wo))
        )
    ]
    for load in loads:
        load.start()

    barrier = pltpu.get_barrier_semaphore()
    pl.semaphore_signal(barrier, inc=1, device_id=peer, device_id_type=MESH)

    def greet(k, carry):
        t = lax.rem(me + k, total)
        pl.semaphore_signal(
            barrier, inc=1, device_id=(lax.rem(t, nseq), c, t // nseq), device_id_type=MESH
        )
        return carry

    lax.fori_loop(1, total, greet, 0)
    pl.semaphore_wait(barrier, total)

    mine = pl.ds(pl.multiple_of(c * half_rows, EDGE), half_rows)
    pool2[mine, :] = pooled[...]
    swap = pltpu.make_async_remote_copy(
        src_ref=pooled,
        dst_ref=pool2.at[mine],
        send_sem=pair_send.at[0],
        recv_sem=pair_recv.at[0],
        device_id=peer,
        device_id_type=MESH,
    )
    swap.start()
    swap.wait()

    values = pool2[...].astype(jnp.float32)
    centred = values - jnp.mean(values, axis=1, keepdims=True)
    spread = jnp.mean(centred * centred, axis=1, keepdims=True)
    normed = centred * lax.rsqrt(spread + 1e-05) * gain[...]
    proj[...] = normed
    inputs = normed.astype(jnp.bfloat16)
    here = pl.ds(pl.multiple_of(s * rows, rows), rows)
    loads[0].wait()
    kv[here, 0:key_cols] = jnp.dot(
        inputs, wk[...], preferred_element_type=jnp.float32
    ).astype(jnp.bfloat16)
    loads[1].wait()
    kv[here, key_cols : key_cols + val_cols] = jnp.dot(
        inputs, wv[...], preferred_element_type=jnp.float32
    ).astype(jnp.bfloat16)

    def kv_copy(k, owner):
        return pltpu.make_async_remote_copy(
            src_ref=kv.at[here],
            dst_ref=kv.at[pl.ds(pl.multiple_of(owner * rows, rows), rows)],
            send_sem=kv_send.at[k],
            recv_sem=kv_recv.at[k],
            device_id=(lax.rem(s + k, nseq), c, b),
            device_id_type=MESH,
        )

    def kv_start(k, carry):
        kv_copy(k, s).start()
        return carry

    def kv_wait(k, carry):
        kv_copy(k, s).wait_send()
        kv_copy(k, lax.rem(s + nseq - k, nseq)).wait_recv()
        return carry

    lax.fori_loop(1, nseq, kv_start, 0)
    loads[2].wait()
    query = (
        jnp.dot(inputs, wq[...], preferred_element_type=jnp.float32) * KEY ** (-0.5)
    ).astype(jnp.bfloat16)
    lax.fori_loop(1, nseq, kv_wait, 0)

    count = kv.shape[0]
    positions = lax.broadcasted_iota(jnp.int32, (rows, count), 1)
    visible = (positions >= lower[...]) & (positions < upper[...])
    lane = lax.broadcasted_iota(jnp.int32, (rows, 128), 1)
    pieces = []
    for pair in range(heads // 2):
        results = []
        for side in range(2):
            h = 2 * pair + side
            scores = lax.dot_general(
                query[:, h * KEY : (h + 1) * KEY],
                kv[:, h * KEY : (h + 1) * KEY],
                (((1,), (1,)), ((), ())),
                preferred_element_type=jnp.float32,
            )
            scores = jnp.where(visible, scores + bias[h], jnp.float32(-1e30))
            newest = jnp.max(scores, axis=1, keepdims=True)
            weights = jnp.where(visible, jnp.exp(scores - newest), jnp.float32(0.0))
            weight_sum = jnp.sum(weights, axis=1, keepdims=True)
            first = key_cols + pair * 2 * VAL + side * 128
            accum = jnp.dot(
                weights.astype(jnp.bfloat16),
                kv[:, first : first + 256],
                preferred_element_type=jnp.float32,
            )
            results.append(accum / weight_sum)
        left, right = results
        pieces += [
            left[:, :128],
            jnp.where(lane < VAL - 128, left[:, 128:], right[:, :128]),
            right[:, 128:],
        ]
    attended = jnp.concatenate(pieces, axis=1).astype(jnp.bfloat16)
    own_rows = pl.ds(pl.multiple_of(me * rows, rows), rows)
    att[own_rows, :] = attended

    def att_copy(k, owner):
        t = lax.rem(me + k, total)
        return pltpu.make_async_remote_copy(
            src_ref=att.at[own_rows],
            dst_ref=att.at[pl.ds(pl.multiple_of(owner * rows, rows), rows)],
            send_sem=att_send.at[k],
            recv_sem=att_recv.at[k],
            device_id=(lax.rem(t, nseq), c, t // nseq),
            device_id_type=MESH,
        )

    def att_start(k, carry):
        att_copy(k, me).start()
        return carry

    def att_wait(k, carry):
        att_copy(k, me).wait_send()
        att_copy(k, lax.rem(me + total - k, total)).wait_recv()
        return carry

    lax.fori_loop(1, total, att_start, 0)
    loads[3].wait()
    own_cols = pl.ds(pl.multiple_of(c * out_cols, 128), out_cols)
    peer_cols = pl.ds(pl.multiple_of((1 - c) * out_cols, 128), out_cols)
    other[0] = jnp.dot(attended, wo[:, peer_cols], preferred_element_type=jnp.float32)
    swap_out = pltpu.make_async_remote_copy(
        src_ref=other.at[0],
        dst_ref=other.at[1],
        send_sem=pair_send.at[1],
        recv_sem=pair_recv.at[1],
        device_id=peer,
        device_id_type=MESH,
    )
    swap_out.start()
    own = jnp.dot(attended, wo[:, own_cols], preferred_element_type=jnp.float32)
    swap_out.wait()
    layer_out[...] = (proj[:, own_cols] + (own + other[1])).astype(jnp.bfloat16)
    lax.fori_loop(1, total, att_wait, 0)


def attention(nseq, nbatch, pooled, gain, wq, wk, wv, wo, bias, lower, upper):
    rows = 2 * pooled.shape[0]
    channels = pooled.shape[1]
    total = nseq * nbatch
    cols = channels // 2
    hbm = pl.BlockSpec(memory_space=pl.ANY)
    vmem = pl.BlockSpec(memory_space=pltpu.VMEM)
    return pl.pallas_call(
        functools.partial(attention_kernel, nseq, nbatch),
        out_shape=(
            jax.ShapeDtypeStruct((rows, cols), jnp.bfloat16),
            jax.ShapeDtypeStruct((total * rows, wv.shape[1]), jnp.bfloat16),
        ),
        in_specs=[vmem, vmem, hbm, hbm, hbm, hbm, vmem, vmem, vmem],
        out_specs=(vmem, vmem),
        scratch_shapes=[
            pltpu.VMEM((rows, channels), jnp.bfloat16),
            pltpu.VMEM(wq.shape, jnp.bfloat16),
            pltpu.VMEM(wk.shape, jnp.bfloat16),
            pltpu.VMEM(wv.shape, jnp.bfloat16),
            pltpu.VMEM(wo.shape, jnp.bfloat16),
            pltpu.VMEM((nseq * rows, wk.shape[1] + wv.shape[1]), jnp.bfloat16),
            pltpu.VMEM((rows, channels), jnp.float32),
            pltpu.VMEM((2, rows, cols), jnp.float32),
            pltpu.SemaphoreType.DMA((4,)),
            pltpu.SemaphoreType.DMA((2,)),
            pltpu.SemaphoreType.DMA((2,)),
            pltpu.SemaphoreType.DMA((nseq,)),
            pltpu.SemaphoreType.DMA((nseq,)),
            pltpu.SemaphoreType.DMA((total,)),
            pltpu.SemaphoreType.DMA((total,)),
        ],
        compiler_params=pltpu.CompilerParams(
            collective_id=1, has_side_effects=True, vmem_limit_bytes=LIMIT
        ),
        cost_estimate=pl.CostEstimate(
            flops=400_000_000, bytes_accessed=9_000_000, transcendentals=20_000
        ),
    )(pooled, gain, wq, wk, wv, wo, bias, lower, upper)


def solution(mesh):
    nseq, nbatch = mesh.shape["seq"], mesh.shape["batch"]

    def shards(
        features,
        dilated_tap_weight,
        strided_weight,
        norm_gain,
        query_weight,
        key_weight,
        value_weight,
        output_weight,
        position_bias,
        interval_start,
        interval_end,
        cotangent,
    ):
        cotangent_all = lax.all_gather(cotangent[0], ("batch", "seq"), axis=0, tiled=True)
        width = features.shape[2]
        pooled = conv(
            nseq,
            features[0],
            dilated_tap_weight.reshape(3 * width, -1),
            strided_weight.reshape(2 * width, -1),
        )
        layer_out, attended = attention(
            nseq,
            nbatch,
            pooled,
            norm_gain[None],
            query_weight,
            key_weight,
            value_weight,
            output_weight,
            position_bias[0],
            interval_start[0][:, None],
            interval_end[0][:, None],
        )
        output_grad = lax.dot_general(
            attended,
            cotangent_all,
            (((0,), (0,)), ((), ())),
            preferred_element_type=jnp.float32,
        )
        return (layer_out[None], output_grad)

    return jax.shard_map(
        shards,
        mesh=mesh,
        in_specs=(
            P("batch", "seq", None),
            P(None, None, "section"),
            P(None, None, "section"),
            P(),
            P(None, "section"),
            P(None, "section"),
            P(None, "section"),
            P("section", None),
            P("batch", "section", "seq", None),
            P("batch", "seq"),
            P("batch", "seq"),
            P("batch", "seq", None),
        ),
        out_specs=(P("batch", "seq", "section"), P("section", None)),
        check_vma=False,
    )
```

```python
import functools

import jax
import jax.numpy as jnp
from jax import lax
from jax.experimental import pallas as pl
from jax.experimental.pallas import tpu as pltpu
from jax.sharding import PartitionSpec as P

KEY = 128
VAL = 192
POOL = 128
STEP = 8
EDGE = 16
MESH = pl.DeviceIdType.MESH
LIMIT = 56 * 1024 * 1024


class Gather:
    def __init__(self, nseq, nbatch, own, dst, rows, sems):
        self.nseq, self.nbatch, self.own, self.dst, self.rows = nseq, nbatch, own, dst, rows
        self.seq_send, self.seq_recv, self.batch_send, self.batch_recv = sems
        self.s = lax.axis_index("seq")
        self.c = lax.axis_index("section")
        self.b = lax.axis_index("batch")

    def slot(self, batch, seq):
        row = pl.multiple_of((batch * self.nseq + seq) * self.rows, self.rows)
        return self.dst.at[pl.ds(row, self.rows)]

    def source(self, k):
        return lax.rem(self.s + self.nseq - k, self.nseq)

    def seq_copy(self, k, owner):
        return pltpu.make_async_remote_copy(
            src_ref=self.own,
            dst_ref=self.slot(self.b, owner),
            send_sem=self.seq_send.at[k],
            recv_sem=self.seq_recv.at[k],
            device_id=(lax.rem(self.s + k, self.nseq), self.c, self.b),
            device_id_type=MESH,
        )

    def batch_copy(self, k, j, owner, src):
        return pltpu.make_async_remote_copy(
            src_ref=src,
            dst_ref=self.slot(owner, self.source(k)),
            send_sem=self.batch_send.at[k * self.nbatch + j],
            recv_sem=self.batch_recv.at[k * self.nbatch + j],
            device_id=(self.s, self.c, lax.rem(self.b + j, self.nbatch)),
            device_id_type=MESH,
        )

    def start(self):
        def seq(k, carry):
            self.seq_copy(k, self.s).start()
            return carry

        def batch(j, carry):
            self.batch_copy(0, j, self.b, self.own).start()
            return carry

        lax.fori_loop(1, self.nseq, seq, 0)
        lax.fori_loop(1, self.nbatch, batch, 0)

    def forward(self):
        def seq(k, carry):
            self.seq_copy(k, self.s).wait_send()
            self.seq_copy(k, self.source(k)).wait_recv()

            def batch(j, inner):
                self.batch_copy(k, j, self.b, self.slot(self.b, self.source(k))).start()
                return inner

            return lax.fori_loop(1, self.nbatch, batch, carry)

        lax.fori_loop(1, self.nseq, seq, 0)

    def finish(self):
        def seq(k, carry):
            def batch(j, inner):
                owner = lax.rem(self.b + self.nbatch - j, self.nbatch)
                self.batch_copy(k, j, self.b, self.own).wait_send()
                self.batch_copy(k, j, owner, self.own).wait_recv()
                return inner

            return lax.fori_loop(1, self.nbatch, batch, carry)

        lax.fori_loop(0, self.nseq, seq, 0)


def gather_semaphores(nseq, nbatch):
    return [pltpu.SemaphoreType.DMA((n,)) for n in (nseq, nseq, nseq * nbatch, nseq * nbatch)]


def enter(nseq, nbatch):
    s, c, b = (lax.axis_index(name) for name in ("seq", "section", "batch"))
    barrier = pltpu.get_barrier_semaphore()
    pl.semaphore_signal(barrier, inc=1, device_id=(s, 1 - c, b), device_id_type=MESH)

    def seq(k, carry):
        device = (lax.rem(s + k, nseq), c, b)
        pl.semaphore_signal(barrier, inc=1, device_id=device, device_id_type=MESH)
        return carry

    def batch(k, carry):
        device = (s, c, lax.rem(b + k, nbatch))
        pl.semaphore_signal(barrier, inc=1, device_id=device, device_id_type=MESH)
        return carry

    lax.fori_loop(1, nseq, seq, 0)
    lax.fori_loop(1, nbatch, batch, 0)
    pl.semaphore_wait(barrier, nseq + nbatch - 1)


def conv_kernel(
    nseq,
    nbatch,
    features,
    dil,
    strd,
    cot,
    out,
    cot_half,
    x,
    wd,
    ws,
    hs,
    hp,
    pooled,
    local_sem,
    send_sem,
    recv_sem,
    *gather_sems,
):
    s = lax.axis_index("seq")
    c = lax.axis_index("section")
    b = lax.axis_index("batch")
    length, width = features.shape
    half_rows = length // 2
    part = dil.shape[1]
    cols = strd.shape[1]
    peer = (s, 1 - c, b)
    halo_target = (lax.rem(s + 1 - 2 * c + nseq, nseq), c, b)

    load_x = pltpu.make_async_copy(
        features.at[pl.ds(pl.multiple_of(c * (half_rows - EDGE), EDGE), half_rows + EDGE)],
        x.at[pl.ds(pl.multiple_of(EDGE * (1 - c), EDGE), half_rows + EDGE)],
        local_sem.at[0],
    )
    load_d = pltpu.make_async_copy(dil, wd.at[0], local_sem.at[1])
    load_s = pltpu.make_async_copy(strd, ws.at[0], local_sem.at[2])
    load_d.start()
    load_x.start()

    enter(nseq, nbatch)

    edge_row = pl.multiple_of(c * (half_rows + EDGE), EDGE)
    halo = pltpu.make_async_remote_copy(
        src_ref=features.at[pl.ds(pl.multiple_of((1 - c) * (length - EDGE), EDGE), EDGE)],
        dst_ref=x.at[pl.ds(edge_row, EDGE)],
        send_sem=send_sem.at[0],
        recv_sem=recv_sem.at[0],
        device_id=halo_target,
        device_id_type=MESH,
    )
    send_d = pltpu.make_async_remote_copy(
        src_ref=dil,
        dst_ref=wd.at[1],
        send_sem=send_sem.at[1],
        recv_sem=recv_sem.at[1],
        device_id=peer,
        device_id_type=MESH,
    )
    send_s = pltpu.make_async_remote_copy(
        src_ref=strd,
        dst_ref=ws.at[1],
        send_sem=send_sem.at[2],
        recv_sem=recv_sem.at[2],
        device_id=peer,
        device_id_type=MESH,
    )
    halo.start()
    send_d.start()
    send_s.start()
    load_s.start()
    cot_rows, cot_cols = cot.shape[0], cot_half.shape[1]
    cot_own = cot.at[:, pl.ds(pl.multiple_of(c * cot_cols, 128), cot_cols)]
    gather = Gather(nseq, nbatch, cot_own, cot_half, cot_rows, gather_sems)
    keep_cot = pltpu.make_async_copy(cot_own, gather.slot(b, s), local_sem.at[3])
    keep_cot.start()
    gather.start()

    load_x.wait()
    load_d.wait()
    halo.wait()
    outside = ((c == 0) & (s == 0)) | ((c == 1) & (s == nseq - 1))
    keep = jnp.where(outside, 0.0, 1.0).astype(jnp.float32)
    edge = x[pl.ds(edge_row, EDGE), :].astype(jnp.float32) * keep
    x[pl.ds(edge_row, EDGE), :] = edge.astype(jnp.bfloat16)

    chunk = hs.shape[2]
    lane_blocks = part // 128

    def dilated(slot, half):
        first = pl.multiple_of(half * part, 128)

        def body(i, carry):
            row = pl.multiple_of(i * chunk, chunk)
            block = x[pl.ds(row, chunk + 2 * EDGE), :]
            taps = jnp.concatenate(
                [block[EDGE + d : EDGE + d + chunk] for d in (-STEP, 0, STEP)], axis=1
            )
            preact = jnp.dot(taps, wd[slot], preferred_element_type=jnp.float32)
            own = x[pl.ds(row + EDGE, chunk), pl.ds(first, part)].astype(jnp.float32)
            hidden = own + jax.nn.gelu(preact)
            at = lax.rem(i, 2)
            for j in range(lane_blocks):
                hs[at, j] = hidden[:, 128 * j : 128 * (j + 1)]
            target = pl.multiple_of(i * (chunk // 2), chunk // 2)
            for parity in range(2):
                for j in range(lane_blocks):
                    lane = pl.multiple_of(first + parity * width + 128 * j, 128)
                    hp[pl.ds(target, chunk // 2), pl.ds(lane, 128)] = hs[
                        at, j, pl.ds(parity, chunk // 2, 2), :
                    ].astype(jnp.bfloat16)
            return carry

        lax.fori_loop(0, half_rows // chunk, body, 0, unroll=2)

    def strided(slot, half):
        rows = 8 * (POOL // 2)
        block_cols = 256
        per = cols // block_cols

        def body(k, carry):
            i, n = k // per, lax.rem(k, per)
            lane = pl.multiple_of(n * block_cols, block_cols)
            product = jnp.dot(
                hp[pl.ds(pl.multiple_of(i * rows, rows), rows), :],
                ws[slot, :, pl.ds(lane, block_cols)],
                preferred_element_type=jnp.float32,
            )
            best = product.reshape(8, POOL // 2, block_cols).max(axis=1)
            pooled[
                pl.ds(pl.multiple_of(i * 8, 8), 8),
                pl.ds(pl.multiple_of(half * cols + lane, 128), block_cols),
            ] = best
            return carry

        lax.fori_loop(0, half_rows // 2 // rows * per, body, 0)

    dilated(0, c)
    send_d.wait()
    gather.forward()
    dilated(1, 1 - c)
    load_s.wait()
    strided(0, c)
    send_s.wait()
    strided(1, 1 - c)
    out[...] = pooled[...].astype(jnp.bfloat16)
    keep_cot.wait()
    gather.finish()


def conv(nseq, nbatch, features, dil, strd, cot):
    length, width = features.shape
    part = dil.shape[1]
    cols = strd.shape[1]
    rows = length // 2 // POOL
    chunk = 256
    hbm = pl.BlockSpec(memory_space=pl.ANY)
    return pl.pallas_call(
        functools.partial(conv_kernel, nseq, nbatch),
        out_shape=(
            jax.ShapeDtypeStruct((rows, 2 * cols), jnp.bfloat16),
            jax.ShapeDtypeStruct((nseq * nbatch * cot.shape[0], cot.shape[1] // 2), jnp.bfloat16),
        ),
        in_specs=[hbm, hbm, hbm, hbm],
        out_specs=(pl.BlockSpec(memory_space=pltpu.VMEM), hbm),
        scratch_shapes=[
            pltpu.VMEM((length // 2 + 2 * EDGE, width), jnp.bfloat16),
            pltpu.VMEM((2,) + dil.shape, jnp.bfloat16),
            pltpu.VMEM((2,) + strd.shape, jnp.bfloat16),
            pltpu.VMEM((2, part // 128, chunk, 128), jnp.float32),
            pltpu.VMEM((length // 4, 2 * width), jnp.bfloat16),
            pltpu.VMEM((rows, 2 * cols), jnp.float32),
            pltpu.SemaphoreType.DMA((4,)),
            pltpu.SemaphoreType.DMA((3,)),
            pltpu.SemaphoreType.DMA((3,)),
        ]
        + gather_semaphores(nseq, nbatch),
        compiler_params=pltpu.CompilerParams(
            collective_id=0, has_side_effects=True, vmem_limit_bytes=LIMIT
        ),
        cost_estimate=pl.CostEstimate(
            flops=12_000_000_000, bytes_accessed=8_000_000, transcendentals=1_600_000
        ),
    )(features, dil, strd, cot)


def attention_kernel(
    nseq,
    nbatch,
    pooled,
    gain,
    query_w,
    key_w,
    value_w,
    output_w,
    bias,
    lower,
    upper,
    cot_half,
    layer_out,
    att,
    cot_all,
    pool2,
    wq,
    wk,
    wv,
    wo,
    kv,
    proj,
    other,
    local_sem,
    pair_send,
    pair_recv,
    kv_send,
    kv_recv,
    *gather_sems,
):
    s = lax.axis_index("seq")
    c = lax.axis_index("section")
    b = lax.axis_index("batch")
    me = b * nseq + s
    half_rows = pooled.shape[0]
    rows = 2 * half_rows
    key_cols = key_w.shape[1]
    val_cols = value_w.shape[1]
    heads = key_cols // KEY
    out_cols = layer_out.shape[1]
    peer = (s, 1 - c, b)

    loads = [
        pltpu.make_async_copy(src, dst, local_sem.at[k])
        for k, (src, dst) in enumerate(
            ((key_w, wk), (value_w, wv), (query_w, wq), (output_w, wo))
        )
    ]
    for load in loads:
        load.start()

    enter(nseq, nbatch)

    mine = pl.ds(pl.multiple_of(c * half_rows, EDGE), half_rows)
    pool2[mine, :] = pooled[...]
    swap = pltpu.make_async_remote_copy(
        src_ref=pooled,
        dst_ref=pool2.at[mine],
        send_sem=pair_send.at[0],
        recv_sem=pair_recv.at[0],
        device_id=peer,
        device_id_type=MESH,
    )
    swap.start()
    cot_cols = cot_half.shape[1]
    cot_place = cot_all.at[:, pl.ds(pl.multiple_of(c * cot_cols, 128), cot_cols)]
    keep_cot = pltpu.make_async_copy(cot_half, cot_place, local_sem.at[4])
    swap_cot = pltpu.make_async_remote_copy(
        src_ref=cot_half,
        dst_ref=cot_place,
        send_sem=pair_send.at[2],
        recv_sem=pair_recv.at[2],
        device_id=peer,
        device_id_type=MESH,
    )
    swap.wait()
    keep_cot.start()
    swap_cot.start()

    values = pool2[...].astype(jnp.float32)
    centred = values - jnp.mean(values, axis=1, keepdims=True)
    spread = jnp.mean(centred * centred, axis=1, keepdims=True)
    normed = centred * lax.rsqrt(spread + 1e-05) * gain[...].reshape(1, -1)
    proj[...] = normed
    inputs = normed.astype(jnp.bfloat16)
    here = pl.ds(pl.multiple_of(s * rows, rows), rows)
    loads[0].wait()
    kv[here, 0:key_cols] = jnp.dot(
        inputs, wk[...], preferred_element_type=jnp.float32
    ).astype(jnp.bfloat16)
    loads[1].wait()
    kv[here, key_cols : key_cols + val_cols] = jnp.dot(
        inputs, wv[...], preferred_element_type=jnp.float32
    ).astype(jnp.bfloat16)

    def kv_copy(k, owner):
        return pltpu.make_async_remote_copy(
            src_ref=kv.at[here],
            dst_ref=kv.at[pl.ds(pl.multiple_of(owner * rows, rows), rows)],
            send_sem=kv_send.at[k],
            recv_sem=kv_recv.at[k],
            device_id=(lax.rem(s + k, nseq), c, b),
            device_id_type=MESH,
        )

    def kv_start(k, carry):
        kv_copy(k, s).start()
        return carry

    def kv_wait(k, carry):
        kv_copy(k, s).wait_send()
        kv_copy(k, lax.rem(s + nseq - k, nseq)).wait_recv()
        return carry

    lax.fori_loop(1, nseq, kv_start, 0)
    loads[2].wait()
    query = (
        jnp.dot(inputs, wq[...], preferred_element_type=jnp.float32) * KEY ** (-0.5)
    ).astype(jnp.bfloat16)
    lax.fori_loop(1, nseq, kv_wait, 0)

    count = kv.shape[0]
    positions = lax.broadcasted_iota(jnp.int32, (rows, count), 1)
    turn = lax.broadcasted_iota(jnp.int32, (rows, rows), 0) == lax.broadcasted_iota(
        jnp.int32, (rows, rows), 1
    )
    low = jnp.sum(jnp.where(turn, lower[...], 0), axis=1, keepdims=True)
    high = jnp.sum(jnp.where(turn, upper[...], 0), axis=1, keepdims=True)
    visible = (positions >= low) & (positions < high)
    lane = lax.broadcasted_iota(jnp.int32, (rows, 128), 1)
    pieces = []
    for pair in range(heads // 2):
        results = []
        for side in range(2):
            h = 2 * pair + side
            scores = lax.dot_general(
                query[:, h * KEY : (h + 1) * KEY],
                kv[:, h * KEY : (h + 1) * KEY],
                (((1,), (1,)), ((), ())),
                preferred_element_type=jnp.float32,
            )
            scores = jnp.where(visible, scores + bias[h], jnp.float32(-1e30))
            newest = jnp.max(scores, axis=1, keepdims=True)
            weights = jnp.where(visible, jnp.exp(scores - newest), jnp.float32(0.0))
            weight_sum = jnp.sum(weights, axis=1, keepdims=True)
            first = key_cols + pair * 2 * VAL + side * 128
            accum = jnp.dot(
                weights.astype(jnp.bfloat16),
                kv[:, first : first + 256],
                preferred_element_type=jnp.float32,
            )
            results.append(accum / weight_sum)
        left, right = results
        pieces += [
            left[:, :128],
            jnp.where(lane < VAL - 128, left[:, 128:], right[:, :128]),
            right[:, 128:],
        ]
    attended = jnp.concatenate(pieces, axis=1).astype(jnp.bfloat16)
    own_rows = pl.ds(pl.multiple_of(me * rows, rows), rows)
    att[own_rows, :] = attended

    gather = Gather(nseq, nbatch, att.at[own_rows], att, rows, gather_sems)
    gather.start()
    loads[3].wait()
    own_cols = pl.ds(pl.multiple_of(c * out_cols, 128), out_cols)
    peer_cols = pl.ds(pl.multiple_of((1 - c) * out_cols, 128), out_cols)
    other[0] = jnp.dot(attended, wo[:, peer_cols], preferred_element_type=jnp.float32)
    swap_out = pltpu.make_async_remote_copy(
        src_ref=other.at[0],
        dst_ref=other.at[1],
        send_sem=pair_send.at[1],
        recv_sem=pair_recv.at[1],
        device_id=peer,
        device_id_type=MESH,
    )
    swap_out.start()
    gather.forward()
    own = jnp.dot(attended, wo[:, own_cols], preferred_element_type=jnp.float32)
    swap_out.wait()
    layer_out[...] = (proj[:, own_cols] + (own + other[1])).astype(jnp.bfloat16)
    keep_cot.wait()
    swap_cot.wait()
    gather.finish()


def attention(nseq, nbatch, pooled, gain, wq, wk, wv, wo, bias, lower, upper, cot_half):
    rows = 2 * pooled.shape[0]
    channels = pooled.shape[1]
    total = nseq * nbatch
    cols = channels // 2
    hbm = pl.BlockSpec(memory_space=pl.ANY)
    vmem = pl.BlockSpec(memory_space=pltpu.VMEM)
    return pl.pallas_call(
        functools.partial(attention_kernel, nseq, nbatch),
        out_shape=(
            jax.ShapeDtypeStruct((rows, cols), jnp.bfloat16),
            jax.ShapeDtypeStruct((total * rows, wv.shape[1]), jnp.bfloat16),
            jax.ShapeDtypeStruct((total * rows, channels), jnp.bfloat16),
        ),
        in_specs=[vmem, vmem, hbm, hbm, hbm, hbm, vmem, vmem, vmem, hbm],
        out_specs=(vmem, vmem, hbm),
        scratch_shapes=[
            pltpu.VMEM((rows, channels), jnp.bfloat16),
            pltpu.VMEM(wq.shape, jnp.bfloat16),
            pltpu.VMEM(wk.shape, jnp.bfloat16),
            pltpu.VMEM(wv.shape, jnp.bfloat16),
            pltpu.VMEM(wo.shape, jnp.bfloat16),
            pltpu.VMEM((nseq * rows, wk.shape[1] + wv.shape[1]), jnp.bfloat16),
            pltpu.VMEM((rows, channels), jnp.float32),
            pltpu.VMEM((2, rows, cols), jnp.float32),
            pltpu.SemaphoreType.DMA((5,)),
            pltpu.SemaphoreType.DMA((3,)),
            pltpu.SemaphoreType.DMA((3,)),
            pltpu.SemaphoreType.DMA((nseq,)),
            pltpu.SemaphoreType.DMA((nseq,)),
        ]
        + gather_semaphores(nseq, nbatch),
        compiler_params=pltpu.CompilerParams(
            collective_id=1, has_side_effects=True, vmem_limit_bytes=LIMIT
        ),
        cost_estimate=pl.CostEstimate(
            flops=400_000_000, bytes_accessed=9_000_000, transcendentals=20_000
        ),
    )(pooled, gain, wq, wk, wv, wo, bias, lower, upper, cot_half)


def solution(mesh):
    nseq, nbatch = mesh.shape["seq"], mesh.shape["batch"]

    def shards(
        features,
        dilated_tap_weight,
        strided_weight,
        norm_gain,
        query_weight,
        key_weight,
        value_weight,
        output_weight,
        position_bias,
        interval_start,
        interval_end,
        cotangent,
    ):
        width = features.shape[2]
        pooled, cot_half = conv(
            nseq,
            nbatch,
            features[0],
            dilated_tap_weight.reshape(3 * width, -1),
            strided_weight.reshape(2 * width, -1),
            cotangent[0],
        )
        layer_out, attended, cotangent_all = attention(
            nseq,
            nbatch,
            pooled,
            norm_gain,
            query_weight,
            key_weight,
            value_weight,
            output_weight,
            position_bias[0],
            interval_start,
            interval_end,
            cot_half,
        )
        output_grad = lax.dot_general(
            attended,
            cotangent_all,
            (((0,), (0,)), ((), ())),
            preferred_element_type=jnp.float32,
        )
        return (layer_out[None], output_grad)

    return jax.shard_map(
        shards,
        mesh=mesh,
        in_specs=(
            P("batch", "seq", None),
            P(None, None, "section"),
            P(None, None, "section"),
            P(),
            P(None, "section"),
            P(None, "section"),
            P(None, "section"),
            P("section", None),
            P("batch", "section", "seq", None),
            P("batch", "seq"),
            P("batch", "seq"),
            P("batch", "seq", None),
        ),
        out_specs=(P("batch", "seq", "section"), P("section", None)),
        check_vma=False,
    )
```

```python
import functools

import jax
import jax.numpy as jnp
from jax import lax
from jax.experimental import pallas as pl
from jax.experimental.pallas import tpu as pltpu
from jax.sharding import PartitionSpec as P

KEY = 128
VAL = 192
POOL = 128
STEP = 8
EDGE = 16
MESH = pl.DeviceIdType.MESH
LIMIT = 56 * 1024 * 1024


class Gather:
    def __init__(self, nseq, nbatch, own, dst, rows, sems, lanes=slice(None)):
        self.lanes = lanes
        self.nseq, self.nbatch, self.own, self.dst, self.rows = nseq, nbatch, own, dst, rows
        self.seq_send, self.seq_recv, self.batch_send, self.batch_recv = sems
        self.s = lax.axis_index("seq")
        self.c = lax.axis_index("section")
        self.b = lax.axis_index("batch")

    def slot(self, batch, seq):
        row = pl.multiple_of((batch * self.nseq + seq) * self.rows, self.rows)
        return self.dst.at[pl.ds(row, self.rows), self.lanes]

    def source(self, k):
        return lax.rem(self.s + self.nseq - k, self.nseq)

    def seq_copy(self, k, owner):
        return pltpu.make_async_remote_copy(
            src_ref=self.own,
            dst_ref=self.slot(self.b, owner),
            send_sem=self.seq_send.at[k],
            recv_sem=self.seq_recv.at[k],
            device_id=(lax.rem(self.s + k, self.nseq), self.c, self.b),
            device_id_type=MESH,
        )

    def batch_copy(self, k, j, owner, src):
        return pltpu.make_async_remote_copy(
            src_ref=src,
            dst_ref=self.slot(owner, self.source(k)),
            send_sem=self.batch_send.at[k * self.nbatch + j],
            recv_sem=self.batch_recv.at[k * self.nbatch + j],
            device_id=(self.s, self.c, lax.rem(self.b + j, self.nbatch)),
            device_id_type=MESH,
        )

    def start(self):
        def seq(k, carry):
            self.seq_copy(k, self.s).start()
            return carry

        def batch(j, carry):
            self.batch_copy(0, j, self.b, self.own).start()
            return carry

        lax.fori_loop(1, self.nseq, seq, 0)
        lax.fori_loop(1, self.nbatch, batch, 0)

    def forward(self):
        def seq(k, carry):
            self.seq_copy(k, self.s).wait_send()
            self.seq_copy(k, self.source(k)).wait_recv()

            def batch(j, inner):
                self.batch_copy(k, j, self.b, self.slot(self.b, self.source(k))).start()
                return inner

            return lax.fori_loop(1, self.nbatch, batch, carry)

        lax.fori_loop(1, self.nseq, seq, 0)

    def finish(self):
        def seq(k, carry):
            def batch(j, inner):
                owner = lax.rem(self.b + self.nbatch - j, self.nbatch)
                self.batch_copy(k, j, self.b, self.own).wait_send()
                self.batch_copy(k, j, owner, self.own).wait_recv()
                return inner

            return lax.fori_loop(1, self.nbatch, batch, carry)

        lax.fori_loop(0, self.nseq, seq, 0)


def gather_semaphores(nseq, nbatch):
    return [pltpu.SemaphoreType.DMA((n,)) for n in (nseq, nseq, nseq * nbatch, nseq * nbatch)]


def enter(nseq, nbatch):
    s, c, b = (lax.axis_index(name) for name in ("seq", "section", "batch"))
    barrier = pltpu.get_barrier_semaphore()
    pl.semaphore_signal(barrier, inc=1, device_id=(s, 1 - c, b), device_id_type=MESH)

    def seq(k, carry):
        device = (lax.rem(s + k, nseq), c, b)
        pl.semaphore_signal(barrier, inc=1, device_id=device, device_id_type=MESH)
        return carry

    def batch(k, carry):
        device = (s, c, lax.rem(b + k, nbatch))
        pl.semaphore_signal(barrier, inc=1, device_id=device, device_id_type=MESH)
        return carry

    lax.fori_loop(1, nseq, seq, 0)
    lax.fori_loop(1, nbatch, batch, 0)
    pl.semaphore_wait(barrier, nseq + nbatch - 1)


def conv_kernel(
    nseq,
    nbatch,
    features,
    dil,
    strd,
    cot,
    out,
    cot_all,
    x,
    wd,
    ws,
    hs,
    hp,
    pooled,
    local_sem,
    send_sem,
    recv_sem,
    *gather_sems,
):
    s = lax.axis_index("seq")
    c = lax.axis_index("section")
    b = lax.axis_index("batch")
    length, width = features.shape
    half_rows = length // 2
    part = dil.shape[1]
    cols = strd.shape[1]
    peer = (s, 1 - c, b)
    halo_target = (lax.rem(s + 1 - 2 * c + nseq, nseq), c, b)

    load_x = pltpu.make_async_copy(
        features.at[pl.ds(pl.multiple_of(c * (half_rows - EDGE), EDGE), half_rows + EDGE)],
        x.at[pl.ds(pl.multiple_of(EDGE * (1 - c), EDGE), half_rows + EDGE)],
        local_sem.at[0],
    )
    load_d = pltpu.make_async_copy(dil, wd.at[0], local_sem.at[1])
    load_s = pltpu.make_async_copy(strd, ws.at[0], local_sem.at[2])
    load_d.start()
    load_x.start()

    enter(nseq, nbatch)

    edge_row = pl.multiple_of(c * (half_rows + EDGE), EDGE)
    halo = pltpu.make_async_remote_copy(
        src_ref=features.at[pl.ds(pl.multiple_of((1 - c) * (length - EDGE), EDGE), EDGE)],
        dst_ref=x.at[pl.ds(edge_row, EDGE)],
        send_sem=send_sem.at[0],
        recv_sem=recv_sem.at[0],
        device_id=halo_target,
        device_id_type=MESH,
    )
    send_d = pltpu.make_async_remote_copy(
        src_ref=dil,
        dst_ref=wd.at[1],
        send_sem=send_sem.at[1],
        recv_sem=recv_sem.at[1],
        device_id=peer,
        device_id_type=MESH,
    )
    send_s = pltpu.make_async_remote_copy(
        src_ref=strd,
        dst_ref=ws.at[1],
        send_sem=send_sem.at[2],
        recv_sem=recv_sem.at[2],
        device_id=peer,
        device_id_type=MESH,
    )
    halo.start()
    send_d.start()
    send_s.start()
    load_s.start()
    cot_rows, cot_cols = cot.shape[0], cot.shape[1] // 2
    cot_lanes = pl.ds(pl.multiple_of(c * cot_cols, 128), cot_cols)
    cot_own = cot.at[:, cot_lanes]
    cot_place = cot_all.at[:, cot_lanes]
    gather = Gather(nseq, nbatch, cot_own, cot_all, cot_rows, gather_sems, cot_lanes)
    swap_cot = pltpu.make_async_remote_copy(
        src_ref=cot_place,
        dst_ref=cot_place,
        send_sem=send_sem.at[3],
        recv_sem=recv_sem.at[3],
        device_id=peer,
        device_id_type=MESH,
    )
    keep_cot = pltpu.make_async_copy(cot_own, gather.slot(b, s), local_sem.at[3])
    keep_cot.start()
    gather.start()

    load_x.wait()
    load_d.wait()
    halo.wait()
    outside = ((c == 0) & (s == 0)) | ((c == 1) & (s == nseq - 1))
    keep = jnp.where(outside, 0.0, 1.0).astype(jnp.float32)
    edge = x[pl.ds(edge_row, EDGE), :].astype(jnp.float32) * keep
    x[pl.ds(edge_row, EDGE), :] = edge.astype(jnp.bfloat16)

    chunk = hs.shape[2]
    lane_blocks = part // 128

    def dilated(slot, half):
        first = pl.multiple_of(half * part, 128)

        def body(i, carry):
            row = pl.multiple_of(i * chunk, chunk)
            block = x[pl.ds(row, chunk + 2 * EDGE), :]
            taps = jnp.concatenate(
                [block[EDGE + d : EDGE + d + chunk] for d in (-STEP, 0, STEP)], axis=1
            )
            preact = jnp.dot(taps, wd[slot], preferred_element_type=jnp.float32)
            own = x[pl.ds(row + EDGE, chunk), pl.ds(first, part)].astype(jnp.float32)
            hidden = own + jax.nn.gelu(preact)
            at = lax.rem(i, 2)
            for j in range(lane_blocks):
                hs[at, j] = hidden[:, 128 * j : 128 * (j + 1)]
            target = pl.multiple_of(i * (chunk // 2), chunk // 2)
            for parity in range(2):
                for j in range(lane_blocks):
                    lane = pl.multiple_of(first + parity * width + 128 * j, 128)
                    hp[pl.ds(target, chunk // 2), pl.ds(lane, 128)] = hs[
                        at, j, pl.ds(parity, chunk // 2, 2), :
                    ].astype(jnp.bfloat16)
            return carry

        lax.fori_loop(0, half_rows // chunk, body, 0, unroll=2)

    def strided(slot, half):
        rows = 8 * (POOL // 2)
        block_cols = 256
        per = cols // block_cols

        def body(k, carry):
            i, n = k // per, lax.rem(k, per)
            lane = pl.multiple_of(n * block_cols, block_cols)
            product = jnp.dot(
                hp[pl.ds(pl.multiple_of(i * rows, rows), rows), :],
                ws[slot, :, pl.ds(lane, block_cols)],
                preferred_element_type=jnp.float32,
            )
            best = product.reshape(8, POOL // 2, block_cols).max(axis=1)
            pooled[
                pl.ds(pl.multiple_of(i * 8, 8), 8),
                pl.ds(pl.multiple_of(half * cols + lane, 128), block_cols),
            ] = best
            return carry

        lax.fori_loop(0, half_rows // 2 // rows * per, body, 0)

    dilated(0, c)
    send_d.wait()
    gather.forward()
    dilated(1, 1 - c)
    keep_cot.wait()
    gather.finish()
    swap_cot.start()
    load_s.wait()
    strided(0, c)
    send_s.wait()
    strided(1, 1 - c)
    out[...] = pooled[...].astype(jnp.bfloat16)
    swap_cot.wait()


def conv(nseq, nbatch, features, dil, strd, cot):
    length, width = features.shape
    part = dil.shape[1]
    cols = strd.shape[1]
    rows = length // 2 // POOL
    chunk = 256
    hbm = pl.BlockSpec(memory_space=pl.ANY)
    return pl.pallas_call(
        functools.partial(conv_kernel, nseq, nbatch),
        out_shape=(
            jax.ShapeDtypeStruct((rows, 2 * cols), jnp.bfloat16),
            jax.ShapeDtypeStruct((nseq * nbatch * cot.shape[0], cot.shape[1]), jnp.bfloat16),
        ),
        in_specs=[hbm, hbm, hbm, hbm],
        out_specs=(pl.BlockSpec(memory_space=pltpu.VMEM), hbm),
        scratch_shapes=[
            pltpu.VMEM((length // 2 + 2 * EDGE, width), jnp.bfloat16),
            pltpu.VMEM((2,) + dil.shape, jnp.bfloat16),
            pltpu.VMEM((2,) + strd.shape, jnp.bfloat16),
            pltpu.VMEM((2, part // 128, chunk, 128), jnp.float32),
            pltpu.VMEM((length // 4, 2 * width), jnp.bfloat16),
            pltpu.VMEM((rows, 2 * cols), jnp.float32),
            pltpu.SemaphoreType.DMA((4,)),
            pltpu.SemaphoreType.DMA((4,)),
            pltpu.SemaphoreType.DMA((4,)),
        ]
        + gather_semaphores(nseq, nbatch),
        compiler_params=pltpu.CompilerParams(
            collective_id=0, has_side_effects=True, vmem_limit_bytes=LIMIT
        ),
        cost_estimate=pl.CostEstimate(
            flops=12_000_000_000, bytes_accessed=8_000_000, transcendentals=1_600_000
        ),
    )(features, dil, strd, cot)


def attention_kernel(
    nseq,
    nbatch,
    pooled,
    gain,
    query_w,
    key_w,
    value_w,
    output_w,
    bias,
    lower,
    upper,
    layer_out,
    att,
    pool2,
    wq,
    wk,
    wv,
    wo,
    kv,
    proj,
    other,
    local_sem,
    pair_send,
    pair_recv,
    kv_send,
    kv_recv,
    *gather_sems,
):
    s = lax.axis_index("seq")
    c = lax.axis_index("section")
    b = lax.axis_index("batch")
    me = b * nseq + s
    half_rows = pooled.shape[0]
    rows = 2 * half_rows
    key_cols = key_w.shape[1]
    val_cols = value_w.shape[1]
    heads = key_cols // KEY
    out_cols = layer_out.shape[1]
    peer = (s, 1 - c, b)

    loads = [
        pltpu.make_async_copy(src, dst, local_sem.at[k])
        for k, (src, dst) in enumerate(
            ((key_w, wk), (value_w, wv), (query_w, wq), (output_w, wo))
        )
    ]
    for load in loads:
        load.start()

    enter(nseq, nbatch)

    mine = pl.ds(pl.multiple_of(c * half_rows, EDGE), half_rows)
    pool2[mine, :] = pooled[...]
    swap = pltpu.make_async_remote_copy(
        src_ref=pooled,
        dst_ref=pool2.at[mine],
        send_sem=pair_send.at[0],
        recv_sem=pair_recv.at[0],
        device_id=peer,
        device_id_type=MESH,
    )
    swap.start()
    swap.wait()

    values = pool2[...].astype(jnp.float32)
    centred = values - jnp.mean(values, axis=1, keepdims=True)
    spread = jnp.mean(centred * centred, axis=1, keepdims=True)
    normed = centred * lax.rsqrt(spread + 1e-05) * gain[...].reshape(1, -1)
    proj[...] = normed
    inputs = normed.astype(jnp.bfloat16)
    here = pl.ds(pl.multiple_of(s * rows, rows), rows)
    loads[0].wait()
    kv[here, 0:key_cols] = jnp.dot(
        inputs, wk[...], preferred_element_type=jnp.float32
    ).astype(jnp.bfloat16)
    loads[1].wait()
    kv[here, key_cols : key_cols + val_cols] = jnp.dot(
        inputs, wv[...], preferred_element_type=jnp.float32
    ).astype(jnp.bfloat16)

    def kv_copy(k, owner):
        return pltpu.make_async_remote_copy(
            src_ref=kv.at[here],
            dst_ref=kv.at[pl.ds(pl.multiple_of(owner * rows, rows), rows)],
            send_sem=kv_send.at[k],
            recv_sem=kv_recv.at[k],
            device_id=(lax.rem(s + k, nseq), c, b),
            device_id_type=MESH,
        )

    def kv_start(k, carry):
        kv_copy(k, s).start()
        return carry

    def kv_wait(k, carry):
        kv_copy(k, s).wait_send()
        kv_copy(k, lax.rem(s + nseq - k, nseq)).wait_recv()
        return carry

    lax.fori_loop(1, nseq, kv_start, 0)
    loads[2].wait()
    query = (
        jnp.dot(inputs, wq[...], preferred_element_type=jnp.float32) * KEY ** (-0.5)
    ).astype(jnp.bfloat16)
    lax.fori_loop(1, nseq, kv_wait, 0)

    count = kv.shape[0]
    positions = lax.broadcasted_iota(jnp.int32, (rows, count), 1)
    turn = lax.broadcasted_iota(jnp.int32, (rows, rows), 0) == lax.broadcasted_iota(
        jnp.int32, (rows, rows), 1
    )
    low = jnp.sum(jnp.where(turn, lower[...], 0), axis=1, keepdims=True)
    high = jnp.sum(jnp.where(turn, upper[...], 0), axis=1, keepdims=True)
    visible = (positions >= low) & (positions < high)
    lane = lax.broadcasted_iota(jnp.int32, (rows, 128), 1)
    pieces = []
    for pair in range(heads // 2):
        results = []
        for side in range(2):
            h = 2 * pair + side
            scores = lax.dot_general(
                query[:, h * KEY : (h + 1) * KEY],
                kv[:, h * KEY : (h + 1) * KEY],
                (((1,), (1,)), ((), ())),
                preferred_element_type=jnp.float32,
            )
            scores = jnp.where(visible, scores + bias[h], jnp.float32(-1e30))
            newest = jnp.max(scores, axis=1, keepdims=True)
            weights = jnp.where(visible, jnp.exp(scores - newest), jnp.float32(0.0))
            weight_sum = jnp.sum(weights, axis=1, keepdims=True)
            first = key_cols + pair * 2 * VAL + side * 128
            accum = jnp.dot(
                weights.astype(jnp.bfloat16),
                kv[:, first : first + 256],
                preferred_element_type=jnp.float32,
            )
            results.append(accum / weight_sum)
        left, right = results
        pieces += [
            left[:, :128],
            jnp.where(lane < VAL - 128, left[:, 128:], right[:, :128]),
            right[:, 128:],
        ]
    attended = jnp.concatenate(pieces, axis=1).astype(jnp.bfloat16)
    own_rows = pl.ds(pl.multiple_of(me * rows, rows), rows)
    att[own_rows, :] = attended

    gather = Gather(nseq, nbatch, att.at[own_rows], att, rows, gather_sems)
    gather.start()
    loads[3].wait()
    own_cols = pl.ds(pl.multiple_of(c * out_cols, 128), out_cols)
    peer_cols = pl.ds(pl.multiple_of((1 - c) * out_cols, 128), out_cols)
    other[0] = jnp.dot(attended, wo[:, peer_cols], preferred_element_type=jnp.float32)
    swap_out = pltpu.make_async_remote_copy(
        src_ref=other.at[0],
        dst_ref=other.at[1],
        send_sem=pair_send.at[1],
        recv_sem=pair_recv.at[1],
        device_id=peer,
        device_id_type=MESH,
    )
    swap_out.start()
    gather.forward()
    own = jnp.dot(attended, wo[:, own_cols], preferred_element_type=jnp.float32)
    swap_out.wait()
    layer_out[...] = (proj[:, own_cols] + (own + other[1])).astype(jnp.bfloat16)
    gather.finish()


def attention(nseq, nbatch, pooled, gain, wq, wk, wv, wo, bias, lower, upper):
    rows = 2 * pooled.shape[0]
    channels = pooled.shape[1]
    total = nseq * nbatch
    cols = channels // 2
    hbm = pl.BlockSpec(memory_space=pl.ANY)
    vmem = pl.BlockSpec(memory_space=pltpu.VMEM)
    return pl.pallas_call(
        functools.partial(attention_kernel, nseq, nbatch),
        out_shape=(
            jax.ShapeDtypeStruct((rows, cols), jnp.bfloat16),
            jax.ShapeDtypeStruct((total * rows, wv.shape[1]), jnp.bfloat16),
        ),
        in_specs=[vmem, vmem, hbm, hbm, hbm, hbm, vmem, vmem, vmem],
        out_specs=(vmem, vmem),
        scratch_shapes=[
            pltpu.VMEM((rows, channels), jnp.bfloat16),
            pltpu.VMEM(wq.shape, jnp.bfloat16),
            pltpu.VMEM(wk.shape, jnp.bfloat16),
            pltpu.VMEM(wv.shape, jnp.bfloat16),
            pltpu.VMEM(wo.shape, jnp.bfloat16),
            pltpu.VMEM((nseq * rows, wk.shape[1] + wv.shape[1]), jnp.bfloat16),
            pltpu.VMEM((rows, channels), jnp.float32),
            pltpu.VMEM((2, rows, cols), jnp.float32),
            pltpu.SemaphoreType.DMA((4,)),
            pltpu.SemaphoreType.DMA((2,)),
            pltpu.SemaphoreType.DMA((2,)),
            pltpu.SemaphoreType.DMA((nseq,)),
            pltpu.SemaphoreType.DMA((nseq,)),
        ]
        + gather_semaphores(nseq, nbatch),
        compiler_params=pltpu.CompilerParams(
            collective_id=1, has_side_effects=True, vmem_limit_bytes=LIMIT
        ),
        cost_estimate=pl.CostEstimate(
            flops=400_000_000, bytes_accessed=9_000_000, transcendentals=20_000
        ),
    )(pooled, gain, wq, wk, wv, wo, bias, lower, upper)


def solution(mesh):
    nseq, nbatch = mesh.shape["seq"], mesh.shape["batch"]

    def shards(
        features,
        dilated_tap_weight,
        strided_weight,
        norm_gain,
        query_weight,
        key_weight,
        value_weight,
        output_weight,
        position_bias,
        interval_start,
        interval_end,
        cotangent,
    ):
        width = features.shape[2]
        pooled, cotangent_all = conv(
            nseq,
            nbatch,
            features[0],
            dilated_tap_weight.reshape(3 * width, -1),
            strided_weight.reshape(2 * width, -1),
            cotangent[0],
        )
        layer_out, attended = attention(
            nseq,
            nbatch,
            pooled,
            norm_gain,
            query_weight,
            key_weight,
            value_weight,
            output_weight,
            position_bias[0],
            interval_start,
            interval_end,
        )
        output_grad = lax.dot_general(
            attended,
            cotangent_all,
            (((0,), (0,)), ((), ())),
            preferred_element_type=jnp.float32,
        )
        return (layer_out[None], output_grad)

    return jax.shard_map(
        shards,
        mesh=mesh,
        in_specs=(
            P("batch", "seq", None),
            P(None, None, "section"),
            P(None, None, "section"),
            P(),
            P(None, "section"),
            P(None, "section"),
            P(None, "section"),
            P("section", None),
            P("batch", "section", "seq", None),
            P("batch", "seq"),
            P("batch", "seq"),
            P("batch", "seq", None),
        ),
        out_specs=(P("batch", "seq", "section"), P("section", None)),
        check_vma=False,
    )
```

```python
import functools

import jax
import jax.numpy as jnp
from jax import lax
from jax.experimental import pallas as pl
from jax.experimental.pallas import tpu as pltpu
from jax.sharding import PartitionSpec as P

KEY = 128
VAL = 192
POOL = 128
STEP = 8
EDGE = 16
MESH = pl.DeviceIdType.MESH
LIMIT = 56 * 1024 * 1024


class Gather:
    def __init__(self, nseq, nbatch, own, dst, rows, sems, lanes=slice(None)):
        self.lanes = lanes
        self.nseq, self.nbatch, self.own, self.dst, self.rows = nseq, nbatch, own, dst, rows
        self.seq_send, self.seq_recv, self.batch_send, self.batch_recv = sems
        self.s = lax.axis_index("seq")
        self.c = lax.axis_index("section")
        self.b = lax.axis_index("batch")

    def slot(self, batch, seq):
        row = pl.multiple_of((batch * self.nseq + seq) * self.rows, self.rows)
        return self.dst.at[pl.ds(row, self.rows), self.lanes]

    def source(self, k):
        return lax.rem(self.s + self.nseq - k, self.nseq)

    def seq_copy(self, k, owner):
        return pltpu.make_async_remote_copy(
            src_ref=self.own,
            dst_ref=self.slot(self.b, owner),
            send_sem=self.seq_send.at[k],
            recv_sem=self.seq_recv.at[k],
            device_id=(lax.rem(self.s + k, self.nseq), self.c, self.b),
            device_id_type=MESH,
        )

    def batch_copy(self, k, j, owner, src):
        return pltpu.make_async_remote_copy(
            src_ref=src,
            dst_ref=self.slot(owner, self.source(k)),
            send_sem=self.batch_send.at[k * self.nbatch + j],
            recv_sem=self.batch_recv.at[k * self.nbatch + j],
            device_id=(self.s, self.c, lax.rem(self.b + j, self.nbatch)),
            device_id_type=MESH,
        )

    def start(self):
        def seq(k, carry):
            self.seq_copy(k, self.s).start()
            return carry

        def batch(j, carry):
            self.batch_copy(0, j, self.b, self.own).start()
            return carry

        lax.fori_loop(1, self.nseq, seq, 0)
        lax.fori_loop(1, self.nbatch, batch, 0)

    def forward(self):
        def seq(k, carry):
            self.seq_copy(k, self.s).wait_send()
            self.seq_copy(k, self.source(k)).wait_recv()

            def batch(j, inner):
                self.batch_copy(k, j, self.b, self.slot(self.b, self.source(k))).start()
                return inner

            return lax.fori_loop(1, self.nbatch, batch, carry)

        lax.fori_loop(1, self.nseq, seq, 0)

    def finish(self):
        def seq(k, carry):
            def batch(j, inner):
                owner = lax.rem(self.b + self.nbatch - j, self.nbatch)
                self.batch_copy(k, j, self.b, self.own).wait_send()
                self.batch_copy(k, j, owner, self.own).wait_recv()
                return inner

            return lax.fori_loop(1, self.nbatch, batch, carry)

        lax.fori_loop(0, self.nseq, seq, 0)


def gather_semaphores(nseq, nbatch):
    return [pltpu.SemaphoreType.DMA((n,)) for n in (nseq, nseq, nseq * nbatch, nseq * nbatch)]


def enter(nseq, nbatch):
    s, c, b = (lax.axis_index(name) for name in ("seq", "section", "batch"))
    barrier = pltpu.get_barrier_semaphore()
    pl.semaphore_signal(barrier, inc=1, device_id=(s, 1 - c, b), device_id_type=MESH)

    def seq(k, carry):
        device = (lax.rem(s + k, nseq), c, b)
        pl.semaphore_signal(barrier, inc=1, device_id=device, device_id_type=MESH)
        return carry

    def batch(k, carry):
        device = (s, c, lax.rem(b + k, nbatch))
        pl.semaphore_signal(barrier, inc=1, device_id=device, device_id_type=MESH)
        return carry

    lax.fori_loop(1, nseq, seq, 0)
    lax.fori_loop(1, nbatch, batch, 0)
    pl.semaphore_wait(barrier, nseq + nbatch - 1)


def conv_kernel(
    nseq,
    nbatch,
    features,
    dil,
    strd,
    cot,
    out,
    cot_all,
    x,
    wd,
    ws,
    hs,
    hp,
    pooled,
    local_sem,
    send_sem,
    recv_sem,
    *gather_sems,
):
    s = lax.axis_index("seq")
    c = lax.axis_index("section")
    b = lax.axis_index("batch")
    length, width = features.shape
    half_rows = length // 2
    part = dil.shape[1]
    cols = strd.shape[1]
    peer = (s, 1 - c, b)
    halo_target = (lax.rem(s + 1 - 2 * c + nseq, nseq), c, b)

    load_x = pltpu.make_async_copy(
        features.at[pl.ds(pl.multiple_of(c * (half_rows - EDGE), EDGE), half_rows + EDGE)],
        x.at[pl.ds(pl.multiple_of(EDGE * (1 - c), EDGE), half_rows + EDGE)],
        local_sem.at[0],
    )
    load_d = pltpu.make_async_copy(dil, wd.at[0], local_sem.at[1])
    load_s = pltpu.make_async_copy(strd, ws.at[0], local_sem.at[2])
    load_d.start()
    load_x.start()

    enter(nseq, nbatch)

    edge_row = pl.multiple_of(c * (half_rows + EDGE), EDGE)
    halo = pltpu.make_async_remote_copy(
        src_ref=features.at[pl.ds(pl.multiple_of((1 - c) * (length - EDGE), EDGE), EDGE)],
        dst_ref=x.at[pl.ds(edge_row, EDGE)],
        send_sem=send_sem.at[0],
        recv_sem=recv_sem.at[0],
        device_id=halo_target,
        device_id_type=MESH,
    )
    send_d = pltpu.make_async_remote_copy(
        src_ref=dil,
        dst_ref=wd.at[1],
        send_sem=send_sem.at[1],
        recv_sem=recv_sem.at[1],
        device_id=peer,
        device_id_type=MESH,
    )
    send_s = pltpu.make_async_remote_copy(
        src_ref=strd,
        dst_ref=ws.at[1],
        send_sem=send_sem.at[2],
        recv_sem=recv_sem.at[2],
        device_id=peer,
        device_id_type=MESH,
    )
    halo.start()
    send_d.start()
    send_s.start()
    load_s.start()
    cot_rows, cot_cols = cot.shape[0], cot.shape[1] // 2
    cot_lanes = pl.ds(pl.multiple_of(c * cot_cols, 128), cot_cols)
    cot_own = cot.at[:, cot_lanes]
    cot_place = cot_all.at[:, cot_lanes]
    gather = Gather(nseq, nbatch, cot_own, cot_all, cot_rows, gather_sems, cot_lanes)
    swap_cot = pltpu.make_async_remote_copy(
        src_ref=cot_place,
        dst_ref=cot_place,
        send_sem=send_sem.at[3],
        recv_sem=recv_sem.at[3],
        device_id=peer,
        device_id_type=MESH,
    )
    keep_cot = pltpu.make_async_copy(cot_own, gather.slot(b, s), local_sem.at[3])
    keep_cot.start()
    gather.start()

    load_x.wait()
    load_d.wait()
    halo.wait()
    outside = ((c == 0) & (s == 0)) | ((c == 1) & (s == nseq - 1))
    keep = jnp.where(outside, 0.0, 1.0).astype(jnp.float32)
    edge = x[pl.ds(edge_row, EDGE), :].astype(jnp.float32) * keep
    x[pl.ds(edge_row, EDGE), :] = edge.astype(jnp.bfloat16)

    chunk = hs.shape[2]
    lane_blocks = part // 128

    def dilated(slot, half):
        first = pl.multiple_of(half * part, 128)

        def body(i, carry):
            row = pl.multiple_of(i * chunk, chunk)
            block = x[pl.ds(row, chunk + 2 * EDGE), :]
            taps = jnp.concatenate(
                [block[EDGE + d : EDGE + d + chunk] for d in (-STEP, 0, STEP)], axis=1
            )
            preact = jnp.dot(taps, wd[slot], preferred_element_type=jnp.float32)
            own = x[pl.ds(row + EDGE, chunk), pl.ds(first, part)].astype(jnp.float32)
            hidden = own + jax.nn.gelu(preact)
            at = lax.rem(i, 2)
            for j in range(lane_blocks):
                hs[at, j] = hidden[:, 128 * j : 128 * (j + 1)]
            target = pl.multiple_of(i * (chunk // 2), chunk // 2)
            for parity in range(2):
                for j in range(lane_blocks):
                    lane = pl.multiple_of(first + parity * width + 128 * j, 128)
                    hp[pl.ds(target, chunk // 2), pl.ds(lane, 128)] = hs[
                        at, j, pl.ds(parity, chunk // 2, 2), :
                    ].astype(jnp.bfloat16)
            return carry

        lax.fori_loop(0, half_rows // chunk, body, 0, unroll=2)

    def strided(slot, half):
        rows = 8 * (POOL // 2)
        block_cols = 256
        per = cols // block_cols

        def body(k, carry):
            i, n = k // per, lax.rem(k, per)
            lane = pl.multiple_of(n * block_cols, block_cols)
            product = jnp.dot(
                hp[pl.ds(pl.multiple_of(i * rows, rows), rows), :],
                ws[slot, :, pl.ds(lane, block_cols)],
                preferred_element_type=jnp.float32,
            )
            best = product.reshape(8, POOL // 2, block_cols).max(axis=1)
            pooled[
                pl.ds(pl.multiple_of(i * 8, 8), 8),
                pl.ds(pl.multiple_of(half * cols + lane, 128), block_cols),
            ] = best
            return carry

        lax.fori_loop(0, half_rows // 2 // rows * per, body, 0)

    dilated(0, c)
    send_d.wait()
    gather.forward()
    dilated(1, 1 - c)
    keep_cot.wait()
    gather.finish()
    swap_cot.start()
    load_s.wait()
    strided(0, c)
    send_s.wait()
    strided(1, 1 - c)
    out[...] = pooled[...].astype(jnp.bfloat16)
    swap_cot.wait()


def conv(nseq, nbatch, features, dil, strd, cot):
    length, width = features.shape
    part = dil.shape[1]
    cols = strd.shape[1]
    rows = length // 2 // POOL
    chunk = 256
    hbm = pl.BlockSpec(memory_space=pl.ANY)
    return pl.pallas_call(
        functools.partial(conv_kernel, nseq, nbatch),
        out_shape=(
            jax.ShapeDtypeStruct((rows, 2 * cols), jnp.bfloat16),
            jax.ShapeDtypeStruct((nseq * nbatch * cot.shape[0], cot.shape[1]), jnp.bfloat16),
        ),
        in_specs=[hbm, hbm, hbm, hbm],
        out_specs=(pl.BlockSpec(memory_space=pltpu.VMEM), hbm),
        scratch_shapes=[
            pltpu.VMEM((length // 2 + 2 * EDGE, width), jnp.bfloat16),
            pltpu.VMEM((2,) + dil.shape, jnp.bfloat16),
            pltpu.VMEM((2,) + strd.shape, jnp.bfloat16),
            pltpu.VMEM((2, part // 128, chunk, 128), jnp.float32),
            pltpu.VMEM((length // 4, 2 * width), jnp.bfloat16),
            pltpu.VMEM((rows, 2 * cols), jnp.float32),
            pltpu.SemaphoreType.DMA((4,)),
            pltpu.SemaphoreType.DMA((4,)),
            pltpu.SemaphoreType.DMA((4,)),
        ]
        + gather_semaphores(nseq, nbatch),
        compiler_params=pltpu.CompilerParams(
            collective_id=0, has_side_effects=True, vmem_limit_bytes=LIMIT
        ),
        cost_estimate=pl.CostEstimate(
            flops=12_000_000_000, bytes_accessed=8_000_000, transcendentals=1_600_000
        ),
    )(features, dil, strd, cot)


def attention_kernel(
    nseq,
    nbatch,
    pooled,
    gain,
    query_w,
    key_w,
    value_w,
    output_w,
    bias,
    lower,
    upper,
    layer_out,
    att,
    pool2,
    wq,
    wk,
    wv,
    wo,
    kv,
    proj,
    other,
    local_sem,
    pair_send,
    pair_recv,
    kv_send,
    kv_recv,
    *gather_sems,
):
    s = lax.axis_index("seq")
    c = lax.axis_index("section")
    b = lax.axis_index("batch")
    me = b * nseq + s
    half_rows = pooled.shape[0]
    rows = 2 * half_rows
    key_cols = key_w.shape[1]
    val_cols = value_w.shape[1]
    heads = key_cols // KEY
    out_cols = layer_out.shape[1]
    peer = (s, 1 - c, b)

    loads = [
        pltpu.make_async_copy(src, dst, local_sem.at[k])
        for k, (src, dst) in enumerate(
            ((key_w, wk), (value_w, wv), (query_w, wq), (output_w, wo))
        )
    ]
    enter(nseq, nbatch)

    mine = pl.ds(pl.multiple_of(c * half_rows, EDGE), half_rows)
    pool2[mine, :] = pooled[...]
    swap = pltpu.make_async_remote_copy(
        src_ref=pooled,
        dst_ref=pool2.at[mine],
        send_sem=pair_send.at[0],
        recv_sem=pair_recv.at[0],
        device_id=peer,
        device_id_type=MESH,
    )
    swap.start()
    for load in loads:
        load.start()
    swap.wait()

    values = pool2[...].astype(jnp.float32)
    centred = values - jnp.mean(values, axis=1, keepdims=True)
    spread = jnp.mean(centred * centred, axis=1, keepdims=True)
    normed = centred * lax.rsqrt(spread + 1e-05) * gain[...].reshape(1, -1)
    proj[...] = normed
    inputs = normed.astype(jnp.bfloat16)
    here = pl.ds(pl.multiple_of(s * rows, rows), rows)
    loads[0].wait()
    kv[here, 0:key_cols] = jnp.dot(
        inputs, wk[...], preferred_element_type=jnp.float32
    ).astype(jnp.bfloat16)
    loads[1].wait()
    kv[here, key_cols : key_cols + val_cols] = jnp.dot(
        inputs, wv[...], preferred_element_type=jnp.float32
    ).astype(jnp.bfloat16)

    def kv_copy(k, owner):
        return pltpu.make_async_remote_copy(
            src_ref=kv.at[here],
            dst_ref=kv.at[pl.ds(pl.multiple_of(owner * rows, rows), rows)],
            send_sem=kv_send.at[k],
            recv_sem=kv_recv.at[k],
            device_id=(lax.rem(s + k, nseq), c, b),
            device_id_type=MESH,
        )

    def kv_start(k, carry):
        kv_copy(k, s).start()
        return carry

    def kv_wait(k, carry):
        kv_copy(k, s).wait_send()
        kv_copy(k, lax.rem(s + nseq - k, nseq)).wait_recv()
        return carry

    lax.fori_loop(1, nseq, kv_start, 0)
    loads[2].wait()
    query = (
        jnp.dot(inputs, wq[...], preferred_element_type=jnp.float32) * KEY ** (-0.5)
    ).astype(jnp.bfloat16)
    lax.fori_loop(1, nseq, kv_wait, 0)

    count = kv.shape[0]
    positions = lax.broadcasted_iota(jnp.int32, (rows, count), 1)
    turn = lax.broadcasted_iota(jnp.int32, (rows, rows), 0) == lax.broadcasted_iota(
        jnp.int32, (rows, rows), 1
    )
    low = jnp.sum(jnp.where(turn, lower[...], 0), axis=1, keepdims=True)
    high = jnp.sum(jnp.where(turn, upper[...], 0), axis=1, keepdims=True)
    visible = (positions >= low) & (positions < high)
    lane = lax.broadcasted_iota(jnp.int32, (rows, 128), 1)
    pieces = []
    for pair in range(heads // 2):
        results = []
        for side in range(2):
            h = 2 * pair + side
            scores = lax.dot_general(
                query[:, h * KEY : (h + 1) * KEY],
                kv[:, h * KEY : (h + 1) * KEY],
                (((1,), (1,)), ((), ())),
                preferred_element_type=jnp.float32,
            )
            scores = jnp.where(visible, scores + bias[h], jnp.float32(-1e30))
            newest = jnp.max(scores, axis=1, keepdims=True)
            weights = jnp.where(visible, jnp.exp(scores - newest), jnp.float32(0.0))
            weight_sum = jnp.sum(weights, axis=1, keepdims=True)
            first = key_cols + pair * 2 * VAL + side * 128
            accum = jnp.dot(
                weights.astype(jnp.bfloat16),
                kv[:, first : first + 256],
                preferred_element_type=jnp.float32,
            )
            results.append(accum / weight_sum)
        left, right = results
        pieces += [
            left[:, :128],
            jnp.where(lane < VAL - 128, left[:, 128:], right[:, :128]),
            right[:, 128:],
        ]
    attended = jnp.concatenate(pieces, axis=1).astype(jnp.bfloat16)
    own_rows = pl.ds(pl.multiple_of(me * rows, rows), rows)
    att[own_rows, :] = attended

    gather = Gather(nseq, nbatch, att.at[own_rows], att, rows, gather_sems)
    gather.start()
    loads[3].wait()
    own_cols = pl.ds(pl.multiple_of(c * out_cols, 128), out_cols)
    peer_cols = pl.ds(pl.multiple_of((1 - c) * out_cols, 128), out_cols)
    other[0] = jnp.dot(attended, wo[:, peer_cols], preferred_element_type=jnp.float32)
    swap_out = pltpu.make_async_remote_copy(
        src_ref=other.at[0],
        dst_ref=other.at[1],
        send_sem=pair_send.at[1],
        recv_sem=pair_recv.at[1],
        device_id=peer,
        device_id_type=MESH,
    )
    swap_out.start()
    own = jnp.dot(attended, wo[:, own_cols], preferred_element_type=jnp.float32)
    gather.forward()
    swap_out.wait()
    layer_out[...] = (proj[:, own_cols] + (own + other[1])).astype(jnp.bfloat16)
    gather.finish()


def attention(nseq, nbatch, pooled, gain, wq, wk, wv, wo, bias, lower, upper):
    rows = 2 * pooled.shape[0]
    channels = pooled.shape[1]
    total = nseq * nbatch
    cols = channels // 2
    hbm = pl.BlockSpec(memory_space=pl.ANY)
    vmem = pl.BlockSpec(memory_space=pltpu.VMEM)
    return pl.pallas_call(
        functools.partial(attention_kernel, nseq, nbatch),
        out_shape=(
            jax.ShapeDtypeStruct((rows, cols), jnp.bfloat16),
            jax.ShapeDtypeStruct((total * rows, wv.shape[1]), jnp.bfloat16),
        ),
        in_specs=[vmem, vmem, hbm, hbm, hbm, hbm, vmem, vmem, vmem],
        out_specs=(vmem, vmem),
        scratch_shapes=[
            pltpu.VMEM((rows, channels), jnp.bfloat16),
            pltpu.VMEM(wq.shape, jnp.bfloat16),
            pltpu.VMEM(wk.shape, jnp.bfloat16),
            pltpu.VMEM(wv.shape, jnp.bfloat16),
            pltpu.VMEM(wo.shape, jnp.bfloat16),
            pltpu.VMEM((nseq * rows, wk.shape[1] + wv.shape[1]), jnp.bfloat16),
            pltpu.VMEM((rows, channels), jnp.float32),
            pltpu.VMEM((2, rows, cols), jnp.float32),
            pltpu.SemaphoreType.DMA((4,)),
            pltpu.SemaphoreType.DMA((2,)),
            pltpu.SemaphoreType.DMA((2,)),
            pltpu.SemaphoreType.DMA((nseq,)),
            pltpu.SemaphoreType.DMA((nseq,)),
        ]
        + gather_semaphores(nseq, nbatch),
        compiler_params=pltpu.CompilerParams(
            collective_id=1, has_side_effects=True, vmem_limit_bytes=LIMIT
        ),
        cost_estimate=pl.CostEstimate(
            flops=400_000_000, bytes_accessed=9_000_000, transcendentals=20_000
        ),
    )(pooled, gain, wq, wk, wv, wo, bias, lower, upper)


def solution(mesh):
    nseq, nbatch = mesh.shape["seq"], mesh.shape["batch"]

    def shards(
        features,
        dilated_tap_weight,
        strided_weight,
        norm_gain,
        query_weight,
        key_weight,
        value_weight,
        output_weight,
        position_bias,
        interval_start,
        interval_end,
        cotangent,
    ):
        width = features.shape[2]
        pooled, cotangent_all = conv(
            nseq,
            nbatch,
            features[0],
            dilated_tap_weight.reshape(3 * width, -1),
            strided_weight.reshape(2 * width, -1),
            cotangent[0],
        )
        layer_out, attended = attention(
            nseq,
            nbatch,
            pooled,
            norm_gain,
            query_weight,
            key_weight,
            value_weight,
            output_weight,
            position_bias[0],
            interval_start,
            interval_end,
        )
        output_grad = lax.dot_general(
            attended,
            cotangent_all,
            (((0,), (0,)), ((), ())),
            preferred_element_type=jnp.float32,
        )
        return (layer_out[None], output_grad)

    return jax.shard_map(
        shards,
        mesh=mesh,
        in_specs=(
            P("batch", "seq", None),
            P(None, None, "section"),
            P(None, None, "section"),
            P(),
            P(None, "section"),
            P(None, "section"),
            P(None, "section"),
            P("section", None),
            P("batch", "section", "seq", None),
            P("batch", "seq"),
            P("batch", "seq"),
            P("batch", "seq", None),
        ),
        out_specs=(P("batch", "seq", "section"), P("section", None)),
        check_vma=False,
    )
```
